32 devices in a mesh: img: 4 (over y, x), ori: 8 (over z, core).
Axes of the slice: x: 2, y: 2, z: 4, core: 2. Of those that a mesh axis runs over, the one named last changes fastest.
Arguments:
- images: bfloat16 [1024, 2, 8192], P('img'), may hold values from -24 to 24
- projections: bfloat16 [1024, 2, 8192], P('ori'), may hold values from -0.2421875 to 0.2421875
- noise_weight: float32 [8192], replicated, may hold values from 0.25 to 4
- shift_ids: int32 [1024, 4], P('img'), may hold values from 0 to 48
- owner_ids: int32 [1024, 64], P('ori', 'img'), may hold values from 0 to 31, as said below
- cell_ids: int32 [1024, 64], P('ori', 'img'), may hold values from 0 to 4095
- weight_ids: int32 [1024, 64], P('ori', 'img'), may hold values from 0 to 63
- interp_table: bfloat16 [64, 128, 128], replicated, may hold values from -0.5 to 0.5
Outputs:
- realspace: float32 [2, 256, 256, 256], P(None, 'img', 'ori')
- loglik: float32 [1024], P('img')
The draws below stay inside these ranges and needn't reach their ends.
Inputs may be any that keep to these rules, and one draw needn't show every extreme that they name: `owner_ids`: among the blocks of one device (rows of one index of ori, columns of one index of img), at most 192 name any one owner; one owner is named exactly 192 times by the blocks of every device.
All inputs are finite; a program needn't handle non-finite values.
Results may differ from the reference program's by a relative error of at most 0.0058.
Values may be sent and summed in bfloat16 or wider, within the bound.
A program may use at most 192 MiB of HBM per device.

```python
import math
import jax
import jax.numpy as jnp
from jax import lax

IMGBOX = 128
K = 8192
LB = 128
BOX = 256
SHIFTS = 4
NTRANS = 49
NWB = 64
ORI_DEV = 128
IMAGES = 1024
ORIENT = 1024
CBLK = 64
CB_DEV = 16
CAP = 192
X_DEV = 32
Y_DEV = 64
ZB = 2
CELLB = 4096
N_IMG = 4
N_ORI = 8
DEVICES = 32


def draw_shared(key):
    shift_table = jax.random.randint(jax.random.fold_in(key, 11), (IMAGES, SHIFTS), 0, NTRANS)
    subkeys = jax.random.split(jax.random.fold_in(key, 12), 3)
    noise_table = jnp.exp(jax.random.uniform(subkeys[0], (K,), jnp.float32, math.log(0.25), math.log(4.0)))
    base_scale = 2.0 / math.sqrt(2 * K)
    image_scale = 0.35
    rising = 0.4 + 0.45 * jnp.arange(ORIENT, dtype=jnp.float32) / max(ORIENT - 1, 1)
    proj_table = jnp.clip(jax.random.normal(subkeys[1], (ORIENT, 2, K), jnp.float32), -4.0, 4.0)
    image_table = jnp.clip(jax.random.normal(subkeys[2], (IMAGES, 2, K), jnp.float32), -4.0, 4.0)
    image_rows = jnp.ones((IMAGES,), jnp.float32)
    proj_table = proj_table * (base_scale * rising)[:, None, None]
    image_table = image_table * (image_scale * image_rows)[:, None, None]
    return (image_table, proj_table, noise_table, shift_table)


def draw_images(key, part):
    return draw_shared(key)[0].astype(jnp.bfloat16)


def draw_projections(key, part):
    return draw_shared(key)[1].astype(jnp.bfloat16)


def draw_noise_weight(key, part):
    return draw_shared(key)[2].astype(jnp.float32)


def draw_shift_ids(key, part):
    return draw_shared(key)[3].astype(jnp.int32)


def draw_owner_ids(key, part):
    slot_count = DEVICES * CAP
    per_device = ORI_DEV * CB_DEV
    boosts = jax.random.randint(jax.random.fold_in(key, 21), (DEVICES,), 0, 4096)
    ranked = boosts * DEVICES + jnp.arange(DEVICES, dtype=jnp.int32)
    favoured = jnp.argmax(ranked)

    def one_source(source):
        source_key = jax.random.fold_in(jax.random.fold_in(key, 22), source)
        noise_int = jax.random.randint(source_key, (DEVICES, CAP), 0, 4096)
        scores = boosts[:, None] * 2 + noise_int
        scores = scores * slot_count + jnp.arange(slot_count, dtype=jnp.int32).reshape(DEVICES, CAP)
        forced = jnp.where(jnp.arange(DEVICES) == favoured, 1073741824, 0).astype(jnp.int32)
        scores = scores + forced[:, None]
        unused, chosen = lax.top_k(scores.reshape(-1), per_device)
        owners = chosen // CAP
        shuffle = jax.random.permutation(jax.random.fold_in(source_key, 1), per_device)
        return owners[shuffle].reshape(ORI_DEV, CB_DEV)
    owner_table = jax.vmap(one_source)(jnp.arange(DEVICES, dtype=jnp.int32))
    owner_table = owner_table.reshape(N_IMG, N_ORI, ORI_DEV, CB_DEV).transpose(1, 2, 0, 3)
    return owner_table.reshape(ORIENT, CBLK).astype(jnp.int32)


def plant(array, rng, smallest, largest):
    spot = [jax.random.randint(jax.random.fold_in(rng, axis), (), 0, length) for axis, length in enumerate(array.shape)]
    longest = array.shape.index(max(array.shape))
    next_to = spot[:longest] + [(spot[longest] + 1) % array.shape[longest]] + spot[longest + 1:]
    return array.at[tuple(spot)].set(smallest).at[tuple(next_to)].set(largest)


def centred(key, dims, width, reach, kind=jnp.bfloat16):
    return jnp.clip(width * jax.random.normal(key, dims, jnp.float32), -reach, reach).astype(kind)


def setup_inputs(seed: int = 0) -> dict:
    streams_of = jax.random.split(jax.random.key(seed), 9)
    return {
        "images": draw_images(jax.random.fold_in(streams_of[8], 71), 0),
        "projections": draw_projections(jax.random.fold_in(streams_of[8], 71), 0),
        "noise_weight": draw_noise_weight(jax.random.fold_in(streams_of[8], 71), 0),
        "shift_ids": draw_shift_ids(jax.random.fold_in(streams_of[8], 71), 0),
        "owner_ids": draw_owner_ids(jax.random.fold_in(streams_of[8], 71), 0),
        "cell_ids": plant(jax.random.randint(streams_of[5], (ORIENT, CBLK), 0, CELLB), jax.random.fold_in(streams_of[5], 1), 0, CELLB - 1).astype(jnp.int32),
        "weight_ids": plant(jax.random.randint(streams_of[6], (ORIENT, CBLK), 0, NWB), jax.random.fold_in(streams_of[6], 1), 0, NWB - 1).astype(jnp.int32),
        "interp_table": centred(streams_of[7], (NWB, LB, LB), LB ** -0.5, 0.5),
    }


def phase_parts(shift_list):
    coef = jnp.arange(K, dtype=jnp.int32)
    kx_index = coef % IMGBOX - IMGBOX // 2
    ky_index = coef // IMGBOX
    shift_x = shift_list % 7 - 3
    shift_y = shift_list // 7 - 3
    phase_turns = (kx_index[None, :] * shift_x[:, None] + ky_index[None, :] * shift_y[:, None]) % IMGBOX
    angles = phase_turns.astype(jnp.float32) * (-2.0 * math.pi / IMGBOX)
    return jnp.cos(angles), jnp.sin(angles)


def aligned_rows(images, shift_ids):
    row_count = images.shape[0]
    cosine, sine_table = phase_parts(shift_ids.reshape(-1).astype(jnp.int32))
    cosine = cosine.reshape(row_count, SHIFTS, K)
    sine_table = sine_table.reshape(row_count, SHIFTS, K)
    real_part = images[:, 0, :].astype(jnp.float32)[:, None, :]
    imag_part = images[:, 1, :].astype(jnp.float32)[:, None, :]
    new_real = real_part * cosine - imag_part * sine_table
    new_imag = real_part * sine_table + imag_part * cosine
    stacked = jnp.stack([new_real, new_imag], axis=2).astype(jnp.bfloat16)
    return stacked.reshape(row_count * SHIFTS, 2 * K)


def reference(images, projections, noise_weight, shift_ids, owner_ids, cell_ids, weight_ids, interp_table):
    aligned = aligned_rows(images, shift_ids)
    proj_float = projections.astype(jnp.float32)
    weighted = (proj_float * noise_weight).astype(jnp.bfloat16).reshape(ORIENT, 2 * K)
    pnorm = jnp.sum(proj_float * proj_float * noise_weight, axis=(1, 2))
    scores = lax.dot_general(aligned, weighted, (((1,), (1,)), ((), ())), preferred_element_type=jnp.float32)
    scores = scores.reshape(IMAGES, SHIFTS, ORIENT) - 0.5 * pnorm
    row_peak = jnp.max(scores, axis=(1, 2))
    row_total = jnp.sum(jnp.exp(scores - row_peak[:, None, None]), axis=(1, 2))
    loglik = row_peak + jnp.log(row_total)
    weights_bf = (jnp.exp(scores - row_peak[:, None, None]) / row_total[:, None, None]).astype(jnp.bfloat16)
    weights_bf = weights_bf.reshape(IMAGES * SHIFTS, ORIENT)
    slices = lax.dot_general(weights_bf, aligned, (((0,), (0,)), ((), ())), preferred_element_type=jnp.float32)
    slices = slices.astype(jnp.bfloat16).reshape(ORIENT, 2, CBLK, LB).transpose(0, 2, 1, 3)

    def block_terms(entries):
        block_values, table_ids = entries
        picked = interp_table[table_ids].astype(jnp.float32)
        return jnp.einsum('cpk,ckj->cpj', block_values.astype(jnp.float32), picked, precision=lax.Precision.HIGHEST)

    contribution = lax.map(block_terms, (slices, weight_ids.astype(jnp.int32)))
    img_index = owner_ids // N_ORI
    ori_index = owner_ids % N_ORI
    pencil = cell_ids // ZB
    half_index = cell_ids % ZB
    x_pos = ori_index * X_DEV + pencil // Y_DEV
    y_pos = img_index * Y_DEV + pencil % Y_DEV
    base_index = (x_pos * BOX + y_pos) * BOX + half_index * LB
    flat_index = (base_index[:, :, None] + jnp.arange(LB, dtype=jnp.int32)[None, None, :]).astype(jnp.int32)
    volume = jnp.zeros((2, BOX * BOX * BOX), jnp.float32)
    volume = volume.at[0, flat_index].add(contribution[:, :, 0, :])
    volume = volume.at[1, flat_index].add(contribution[:, :, 1, :])
    volume = volume.reshape(2, BOX, BOX, BOX)
    transformed = jnp.fft.ifftn(volume[0] + 1j * volume[1], norm="ortho")
    real_out = jnp.transpose(jnp.real(transformed), (2, 1, 0)).astype(jnp.float32)
    imag_out = jnp.transpose(jnp.imag(transformed), (2, 1, 0)).astype(jnp.float32)
    realspace = jnp.stack([real_out, imag_out])
    return realspace, loglik
```

```python
import functools
import math

import jax
import jax.numpy as jnp
import ml_dtypes
import numpy as np
from jax import lax
from jax.experimental import pallas as pl
from jax.experimental.pallas import tpu as pltpu
from jax.sharding import PartitionSpec as P

IMGBOX = 128
BOX = 256
GRID = 7
VMEM_BYTES = 56 * 1024 * 1024
F32 = jnp.float32
BF16 = jnp.bfloat16


def split_table(table, terms):
    rest = table.astype(np.float32)
    pieces = []
    for _ in range(terms):
        piece = rest.astype(ml_dtypes.bfloat16)
        pieces.append(piece)
        rest = rest - piece.astype(np.float32)
    return pieces


def phase_tables(coef_count):
    coef = np.arange(coef_count)
    kx, ky = coef % IMGBOX - IMGBOX // 2, coef // IMGBOX
    shift = np.arange(64)
    dx, dy = shift % GRID - GRID // 2, shift // GRID - GRID // 2
    turns = (kx[None, :] * dx[:, None] + ky[None, :] * dy[:, None]) % IMGBOX
    angles = turns * (-2.0 * math.pi / IMGBOX)
    return (
        np.concatenate(split_table(np.cos(angles), 3)),
        np.concatenate(split_table(np.sin(angles), 3)),
    )


def dft_tables():
    index = np.arange(BOX)
    angles = (index[:, None] * index[None, :] % BOX) * (2.0 * math.pi / BOX)
    factor = 1.0 / math.sqrt(BOX)
    return np.cos(angles) * factor, np.sin(angles) * factor


def z_tables(block_len, chunks):
    cosine, sine = dft_tables()
    span = BOX // chunks
    full = np.zeros((2, BOX, chunks, 2, span))
    cos_c, sin_c = cosine.reshape(BOX, chunks, span), sine.reshape(BOX, chunks, span)
    full[0, :, :, 0], full[0, :, :, 1] = cos_c, sin_c
    full[1, :, :, 0], full[1, :, :, 1] = -sin_c, cos_c
    full = full.reshape(2, BOX // block_len, block_len, 2 * BOX).transpose(1, 0, 2, 3)
    full = full.reshape(BOX // block_len, 2 * block_len, 2 * BOX)
    return np.stack(split_table(full, 2), axis=1)


def cos_sin_split():
    cosine, sine = dft_tables()
    return np.stack(split_table(cosine, 2) + split_table(sine, 2))


def turn_table(width):
    half = width // 2
    table = np.zeros((width, width), np.float32)
    for j in range(half):
        table[j, half + j] = 1.0
        table[half + j, j] = -1.0
    return table.astype(ml_dtypes.bfloat16)


def dot(left, right):
    return jnp.dot(left, right, preferred_element_type=F32)


def params():
    return pltpu.CompilerParams(vmem_limit_bytes=VMEM_BYTES)


def aligned_chunk(pick, cos_ref, sin_ref, img_ref):
    cosine = dot(pick, cos_ref[...])
    sine = dot(pick, sin_ref[...])
    real = img_ref[0].astype(F32)
    imag = img_ref[1].astype(F32)
    new_real = (real * cosine - imag * sine).astype(BF16)
    new_imag = (real * sine + imag * cosine).astype(BF16)
    return new_real, new_imag


def score_kernel(steps, pick_ref, cos_ref, sin_ref, img_ref, proj_ref, noise_ref, out_ref, norm):
    step = pl.program_id(0)
    rows = img_ref.shape[1]
    chunk = img_ref.shape[2]

    @pl.when(step == 0)
    def _():
        out_ref[...] = jnp.zeros_like(out_ref)
        norm[...] = jnp.zeros_like(norm)

    noise = noise_ref[...]
    weighted = []
    for part in range(2):
        proj = proj_ref[part].astype(F32)
        scaled = proj * noise
        weighted.append(scaled.astype(BF16))
        power = scaled * proj
        for lane in range(0, chunk, 128):
            norm[...] += power[:, lane : lane + 128]
    dims = (((1,), (1,)), ((), ()))
    for group in range(pick_ref.shape[0] // rows):
        span = pl.ds(group * rows, rows)
        real, imag = aligned_chunk(pick_ref[span, :], cos_ref, sin_ref, img_ref)
        out_ref[span, :] += lax.dot_general(
            real, weighted[0], dims, preferred_element_type=F32
        ) + lax.dot_general(imag, weighted[1], dims, preferred_element_type=F32)

    @pl.when(step == steps - 1)
    def _():
        out_ref[...] -= 0.5 * jnp.sum(norm[...].T, axis=0, keepdims=True)


def slice_kernel(pick_ref, cos_ref, sin_ref, img_ref, prob_ref, out_ref):
    rows = img_ref.shape[1]
    block_len = out_ref.shape[3]
    totals = [0.0, 0.0]
    for group in range(pick_ref.shape[0] // rows):
        span = pl.ds(group * rows, rows)
        pair = aligned_chunk(pick_ref[span, :], cos_ref, sin_ref, img_ref)
        prob = prob_ref[:, span]
        totals = [total + dot(prob, value) for total, value in zip(totals, pair)]
    for part in range(2):
        for block in range(out_ref.shape[0]):
            piece = totals[part][:, block * block_len : (block + 1) * block_len]
            out_ref[block, part] = piece.astype(BF16)


def place_kernel(tables, group, value_ref, id_ref, table_ref, slot_ref, out_ref, terms):
    step = pl.program_id(0)
    blocks, _, orient, block_len = value_ref.shape
    batch = 8

    @pl.when(step == 0)
    def _():
        @pl.loop(0, blocks // group)
        def _(index):
            span = pl.ds(index * group, group)
            values = value_ref[span].reshape(group * 2 * orient, block_len)
            ids = id_ref[span].reshape(group * 2 * orient, block_len)
            total = jnp.zeros(values.shape, F32)
            for first in range(0, tables, batch):
                picked = [
                    jnp.where(ids == jnp.asarray(w, BF16), values, jnp.zeros_like(values))
                    for w in range(first, first + batch)
                ]
                total += dot(
                    jnp.concatenate(picked, axis=1),
                    table_ref[first * block_len : (first + batch) * block_len, :],
                )
            total = total.astype(BF16).reshape(group, 2, orient, block_len)
            for block in range(group):
                place = pl.multiple_of((index * group + block) * orient, orient)
                for part in range(2):
                    lanes = slice(part * block_len, (part + 1) * block_len)
                    terms[pl.ds(place, orient), lanes] = total[block, part]

    rows = out_ref.shape[0]
    wanted = lax.broadcasted_iota(jnp.int32, (rows, terms.shape[0]), 0) + step * rows
    hit = jnp.where(wanted == slot_ref[...], 1.0, 0.0).astype(BF16)
    out_ref[...] = dot(hit, terms[...]).astype(BF16)


def volume_kernel(depth, cell_ref, term_ref, dft_ref, out_ref):
    step = pl.program_id(0)
    chunks, rows, width = out_ref.shape
    z_blocks = dft_ref.shape[0]
    first = (lax.broadcasted_iota(jnp.int32, (rows, depth), 0) + step * rows) * z_blocks
    result = jnp.zeros((rows, chunks * width), F32)
    for half in range(z_blocks):
        total = jnp.zeros((rows, term_ref.shape[1]), F32)
        for start in range(0, term_ref.shape[0], depth):
            hit = jnp.where(first + half == cell_ref[:, start : start + depth], 1.0, 0.0)
            total += dot(hit.astype(BF16), term_ref[start : start + depth, :])
        total = total.astype(BF16)
        result += dot(total, dft_ref[half, 0]) + dot(total, dft_ref[half, 1])
    for chunk in range(chunks):
        out_ref[chunk] = result[:, chunk * width : (chunk + 1) * width].astype(BF16)


def y_kernel(dft_ref, turn_ref, in_ref, out_ref):
    sources, tall, width = in_ref.shape
    targets, count, span, _ = out_ref.shape
    y_span = tall // count
    plain, turned = [], []
    for x in range(count):
        column = jnp.concatenate(
            [in_ref[source, x * y_span : (x + 1) * y_span, :] for source in range(sources)], axis=0
        )
        plain.append(column)
        turned.append(dot(column, turn_ref[...]).astype(BF16))
    plain = jnp.concatenate(plain, axis=1)
    turned = jnp.concatenate(turned, axis=1)
    result = dot(dft_ref[0], plain) + dot(dft_ref[1], plain)
    result += dot(dft_ref[2], turned) + dot(dft_ref[3], turned)
    for x in range(count):
        for target in range(targets):
            out_ref[target, x] = result[
                target * span : (target + 1) * span, x * width : (x + 1) * width
            ].astype(BF16)


def x_kernel(dft_ref, in_ref, out_ref, wide, left):
    box, count, width = in_ref.shape
    half = width // 2
    wide[...] = in_ref[...].astype(F32)
    for y in range(count):
        row = wide[:, y, :].T
        left[0, y * width : (y + 1) * width, :] = row.astype(BF16)
        left[1, y * width : (y + 1) * width, :] = jnp.concatenate(
            [-row[half:], row[:half]], axis=0
        ).astype(BF16)
    result = dot(left[0], dft_ref[0]) + dot(left[0], dft_ref[1])
    result += dot(left[1], dft_ref[2]) + dot(left[1], dft_ref[3])
    for y in range(count):
        out_ref[:, y, :] = result[y * width : (y + 1) * width, :]


def whole(shape):
    return pl.BlockSpec(shape, lambda i: (0,) * len(shape))


def combine(pairs):
    peaks, totals = pairs[:, 0], pairs[:, 1]
    peak = jnp.max(peaks, axis=0)
    return peak, jnp.sum(totals * jnp.exp(peaks - peak), axis=0)


def local(
    images, projections, noise_weight, shift_ids, owner_ids, cell_ids, weight_ids, interp_table
):
    n_img, n_ori = lax.axis_size("img"), lax.axis_size("ori")
    devices = n_img * n_ori
    row_count, _, coef_count = images.shape
    shift_count = shift_ids.shape[1]
    orient = projections.shape[0]
    tables, block_len, _ = interp_table.shape
    rows = row_count * shift_count
    blocks = owner_ids.shape[1]
    block_count = orient * blocks
    capacity = max(2, (3 * block_count + devices - 1) // devices)
    slots = devices * capacity

    owners = owner_ids.T.reshape(-1)
    cells = cell_ids.T.reshape(-1)
    group = math.gcd(block_count, 128)
    named = owners[:, None] == jnp.arange(devices, dtype=jnp.int32)[None, :]
    named_b = named.astype(BF16).reshape(-1, group, devices)
    lower = jnp.tril(jnp.ones((group, group), BF16))
    within = jnp.einsum("ij,gjd->gid", lower, named_b, preferred_element_type=F32)
    before = jnp.cumsum(within[:, -1], axis=0) - within[:, -1]
    running = (within + before[:, None, :]).reshape(block_count, devices)
    rank = jnp.sum(jnp.where(named, running, 0.0), axis=1).astype(jnp.int32) - 1
    slot_ids = owners * capacity + rank
    send_cells = (
        jnp.full((slots,), -1, jnp.int32).at[slot_ids].set(cells).reshape(devices, capacity)
    )
    got_cells = lax.all_to_all(
        send_cells, ("img", "ori"), split_axis=0, concat_axis=0, tiled=True
    ).reshape(1, slots)
    ids = jnp.broadcast_to(
        weight_ids.T.astype(BF16)[:, None, :, None], (blocks, 2, orient, block_len)
    )

    chunk = math.gcd(coef_count, 1024)
    steps = coef_count // chunk
    cos_table, sin_table = phase_tables(coef_count)
    depth = cos_table.shape[0]
    pick = (
        shift_ids.T.reshape(-1)[:, None] == jnp.arange(depth, dtype=jnp.int32)[None, :] % 64
    ).astype(BF16)
    image_parts = images.transpose(1, 0, 2)
    proj_parts = projections.transpose(1, 0, 2)
    table_spec = pl.BlockSpec((depth, chunk), lambda i: (0, i))
    image_spec = pl.BlockSpec((2, row_count, chunk), lambda i: (0, 0, i))
    scores = pl.pallas_call(
        functools.partial(score_kernel, steps),
        grid=(steps,),
        out_shape=jax.ShapeDtypeStruct((rows, orient), F32),
        in_specs=[
            whole((rows, depth)),
            table_spec,
            table_spec,
            image_spec,
            pl.BlockSpec((2, orient, chunk), lambda i: (0, 0, i)),
            pl.BlockSpec((1, chunk), lambda i: (0, i)),
        ],
        out_specs=whole((rows, orient)),
        scratch_shapes=[pltpu.VMEM((orient, 128), F32)],
        compiler_params=params(),
        name="scores",
    )(pick, cos_table, sin_table, image_parts, proj_parts, noise_weight.reshape(1, -1))
    scores = scores.reshape(shift_count, row_count, orient)
    local_peak = jnp.max(scores, axis=(0, 2))
    local_total = jnp.sum(jnp.exp(scores - local_peak[None, :, None]), axis=(0, 2))
    peak, total = combine(lax.all_gather(jnp.stack([local_peak, local_total]), "ori"))
    loglik = peak + jnp.log(total)
    prob = (jnp.exp(scores - peak[None, :, None]) / total[None, :, None]).astype(BF16)
    prob = prob.reshape(rows, orient).T

    per_step = chunk // block_len
    partial_sums = pl.pallas_call(
        slice_kernel,
        grid=(steps,),
        out_shape=jax.ShapeDtypeStruct((coef_count // block_len, 2, orient, block_len), BF16),
        in_specs=[
            whole((rows, depth)),
            table_spec,
            table_spec,
            image_spec,
            whole((orient, rows)),
        ],
        out_specs=pl.BlockSpec((per_step, 2, orient, block_len), lambda i: (i, 0, 0, 0)),
        compiler_params=params(),
        name="slices",
    )(pick, cos_table, sin_table, image_parts, prob)
    slices = lax.psum_scatter(partial_sums, "img", scatter_dimension=0, tiled=True)

    tile = math.gcd(slots, 512)
    value_shape = (blocks, 2, orient, block_len)
    send_terms = pl.pallas_call(
        functools.partial(place_kernel, tables, math.gcd(blocks, 4)),
        grid=(slots // tile,),
        out_shape=jax.ShapeDtypeStruct((slots, 2 * block_len), BF16),
        in_specs=[
            whole(value_shape),
            whole(value_shape),
            whole((tables * block_len, block_len)),
            whole((1, block_count)),
        ],
        out_specs=pl.BlockSpec((tile, 2 * block_len), lambda i: (i, 0)),
        scratch_shapes=[pltpu.VMEM((block_count, 2 * block_len), BF16)],
        compiler_params=params(),
        name="place",
    )(
        slices,
        ids,
        interp_table.reshape(tables * block_len, block_len),
        slot_ids.reshape(1, block_count),
    )
    got_terms = lax.all_to_all(
        send_terms.reshape(devices, capacity, 2 * block_len),
        ("img", "ori"),
        split_axis=0,
        concat_axis=0,
        tiled=True,
    ).reshape(slots, 2 * block_len)

    x_span, y_span = BOX // n_ori, BOX // n_img
    pencils = x_span * y_span
    width = 2 * (BOX // n_img)
    z_table = z_tables(block_len, n_img)
    tile = math.gcd(pencils, 256)
    pencil_parts = pl.pallas_call(
        functools.partial(volume_kernel, math.gcd(slots, 2048)),
        grid=(pencils // tile,),
        out_shape=jax.ShapeDtypeStruct((n_img, pencils, width), BF16),
        in_specs=[whole((1, slots)), whole((slots, 2 * block_len)), whole(z_table.shape)],
        out_specs=pl.BlockSpec((n_img, tile, width), lambda i: (0, i, 0)),
        compiler_params=params(),
        name="volume",
    )(got_cells, got_terms, z_table)
    pencil_parts = lax.all_to_all(pencil_parts, "img", split_axis=0, concat_axis=0, tiled=True)

    dft = cos_sin_split()
    count = math.gcd(x_span, 4)
    pencil_parts = pl.pallas_call(
        y_kernel,
        grid=(x_span // count,),
        out_shape=jax.ShapeDtypeStruct((n_ori, x_span, BOX // n_ori, width), BF16),
        in_specs=[
            whole(dft.shape),
            whole((width, width)),
            pl.BlockSpec((n_img, count * y_span, width), lambda i: (0, i, 0)),
        ],
        out_specs=pl.BlockSpec((n_ori, count, BOX // n_ori, width), lambda i: (0, i, 0, 0)),
        compiler_params=params(),
        name="along_y",
    )(dft, turn_table(width), pencil_parts)
    pencil_parts = lax.all_to_all(pencil_parts, "ori", split_axis=0, concat_axis=0, tiled=True)

    y_out = BOX // n_ori
    count = math.gcd(y_out, 16)
    realspace = pl.pallas_call(
        x_kernel,
        grid=(y_out // count,),
        out_shape=jax.ShapeDtypeStruct((width, y_out, BOX), F32),
        in_specs=[
            whole(dft.shape),
            pl.BlockSpec((BOX, count, width), lambda i: (0, i, 0)),
        ],
        out_specs=pl.BlockSpec((width, count, BOX), lambda i: (0, i, 0)),
        scratch_shapes=[
            pltpu.VMEM((BOX, count, width), F32),
            pltpu.VMEM((2, count * width, BOX), BF16),
        ],
        compiler_params=params(),
        name="along_x",
    )(dft, pencil_parts.reshape(BOX, y_out, width))
    return realspace.reshape(2, width // 2, y_out, BOX), loglik


def solution(mesh):
    placed = (
        P("img", None, None),
        P("ori", None, None),
        P(),
        P("img", None),
        P("ori", "img"),
        P("ori", "img"),
        P("ori", "img"),
        P(),
    )
    return jax.shard_map(
        local,
        mesh=mesh,
        in_specs=placed,
        out_specs=(P(None, "img", "ori", None), P("img")),
        check_vma=False,
    )
```

```python
import functools
import math

import jax
import jax.numpy as jnp
import ml_dtypes
import numpy as np
from jax import lax
from jax.experimental import pallas as pl
from jax.experimental.pallas import tpu as pltpu
from jax.sharding import PartitionSpec as P

IMGBOX = 128
BOX = 256
GRID = 7
VMEM_BYTES = 56 * 1024 * 1024
F32 = jnp.float32
BF16 = jnp.bfloat16
MESH = pl.DeviceIdType.MESH


def split_table(table, terms):
    rest = table.astype(np.float32)
    pieces = []
    for _ in range(terms):
        piece = rest.astype(ml_dtypes.bfloat16)
        pieces.append(piece)
        rest = rest - piece.astype(np.float32)
    return pieces


def phase_tables(coef_count):
    coef = np.arange(coef_count)
    kx, ky = coef % IMGBOX - IMGBOX // 2, coef // IMGBOX
    shift = np.arange(64)
    dx, dy = shift % GRID - GRID // 2, shift // GRID - GRID // 2
    turns = (kx[None, :] * dx[:, None] + ky[None, :] * dy[:, None]) % IMGBOX
    angles = turns * (-2.0 * math.pi / IMGBOX)
    return (
        np.concatenate(split_table(np.cos(angles), 3)),
        np.concatenate(split_table(np.sin(angles), 3)),
    )


def dft_tables():
    index = np.arange(BOX)
    angles = (index[:, None] * index[None, :] % BOX) * (2.0 * math.pi / BOX)
    factor = 1.0 / math.sqrt(BOX)
    return np.cos(angles) * factor, np.sin(angles) * factor


def z_tables(block_len, chunks):
    cosine, sine = dft_tables()
    span = BOX // chunks
    full = np.zeros((2, BOX, chunks, 2, span))
    cos_c, sin_c = cosine.reshape(BOX, chunks, span), sine.reshape(BOX, chunks, span)
    full[0, :, :, 0], full[0, :, :, 1] = cos_c, sin_c
    full[1, :, :, 0], full[1, :, :, 1] = -sin_c, cos_c
    full = full.reshape(2, BOX // block_len, block_len, 2 * BOX).transpose(1, 0, 2, 3)
    full = full.reshape(BOX // block_len, 2 * block_len, 2 * BOX)
    return np.stack(split_table(full, 2), axis=1)


def cos_sin_split():
    cosine, sine = dft_tables()
    return np.stack(split_table(cosine, 2) + split_table(sine, 2))


def turn_table(width):
    half = width // 2
    table = np.zeros((width, width), np.float32)
    for j in range(half):
        table[j, half + j] = 1.0
        table[half + j, j] = -1.0
    return table.astype(ml_dtypes.bfloat16)


def dot(left, right):
    return jnp.dot(left, right, preferred_element_type=F32)


def params(**more):
    return pltpu.CompilerParams(vmem_limit_bytes=VMEM_BYTES, **more)


def cost(flops, moved):
    return pl.CostEstimate(flops=flops, bytes_accessed=moved, transcendentals=0)


def aligned_chunk(pick, cos_ref, sin_ref, img_ref):
    cosine = dot(pick, cos_ref[...])
    sine = dot(pick, sin_ref[...])
    real = img_ref[0].astype(F32)
    imag = img_ref[1].astype(F32)
    new_real = (real * cosine - imag * sine).astype(BF16)
    new_imag = (real * sine + imag * cosine).astype(BF16)
    return new_real, new_imag


def score_kernel(
    steps, pick_ref, cos_ref, sin_ref, img_ref, proj_ref, noise_ref, out_ref, aligned_ref, norm
):
    step = pl.program_id(0)
    rows = img_ref.shape[1]
    chunk = img_ref.shape[2]

    @pl.when(step == 0)
    def _():
        out_ref[...] = jnp.zeros_like(out_ref)
        norm[...] = jnp.zeros_like(norm)

    noise = noise_ref[...]
    weighted = []
    for part in range(2):
        proj = proj_ref[part].astype(F32)
        scaled = proj * noise
        weighted.append(scaled.astype(BF16))
        power = scaled * proj
        for lane in range(0, chunk, 128):
            norm[...] += power[:, lane : lane + 128]
    dims = (((1,), (1,)), ((), ()))
    for group in range(pick_ref.shape[0] // rows):
        span = pl.ds(group * rows, rows)
        real, imag = aligned_chunk(pick_ref[span, :], cos_ref, sin_ref, img_ref)
        aligned_ref[0, span, :] = real
        aligned_ref[1, span, :] = imag
        out_ref[span, :] += lax.dot_general(
            real, weighted[0], dims, preferred_element_type=F32
        ) + lax.dot_general(imag, weighted[1], dims, preferred_element_type=F32)

    @pl.when(step == steps - 1)
    def _():
        out_ref[...] -= 0.5 * jnp.sum(norm[...].T, axis=0, keepdims=True)


def slice_kernel(aligned_ref, prob_ref, out_ref):
    block_len = out_ref.shape[3]
    for part in range(2):
        total = dot(prob_ref[...], aligned_ref[part])
        for block in range(out_ref.shape[0]):
            piece = total[:, block * block_len : (block + 1) * block_len]
            out_ref[block, part] = piece.astype(BF16)


def interp_kernel(tables, value_ref, id_ref, table_ref, out_ref):
    group, _, orient, block_len = value_ref.shape
    batch = math.gcd(tables, 8)
    values = value_ref[...].reshape(group * 2 * orient, block_len)
    ids = id_ref[...].reshape(group * 2 * orient, block_len)
    total = jnp.zeros(values.shape, F32)
    for first in range(0, tables, batch):
        picked = [
            jnp.where(ids == jnp.asarray(w, BF16), values, jnp.zeros_like(values))
            for w in range(first, first + batch)
        ]
        total += dot(
            jnp.concatenate(picked, axis=1),
            table_ref[first * block_len : (first + batch) * block_len, :],
        )
    total = total.astype(BF16).reshape(group, 2, orient, block_len)
    for block in range(group):
        for part in range(2):
            lanes = slice(part * block_len, (part + 1) * block_len)
            out_ref[block * orient : (block + 1) * orient, lanes] = total[block, part]


def place_kernel(slot_ref, first_ref, second_ref, out_ref):
    step = pl.program_id(0)
    rows = out_ref.shape[0]
    half = first_ref.shape[0]
    wanted = lax.broadcasted_iota(jnp.int32, (rows, half), 0) + step * rows
    total = jnp.zeros(out_ref.shape, F32)
    for index, ref in enumerate((first_ref, second_ref)):
        slots = slot_ref[:, index * half : (index + 1) * half]
        total += dot(jnp.where(wanted == slots, 1.0, 0.0).astype(BF16), ref[...])
    out_ref[...] = total.astype(BF16)


def transform_kernel(
    n_img,
    n_ori,
    count,
    depth,
    cell_ref,
    term_ref,
    z_ref,
    dft_ref,
    turn_ref,
    out_ref,
    to_img,
    from_img,
    to_ori,
    img_send,
    img_recv,
    ori_send,
    ori_recv,
    own_sem,
):
    my_img, my_ori = lax.axis_index("img"), lax.axis_index("ori")
    _, pencils, width = to_img.shape
    x_span, y_out = to_ori.shape[1], to_ori.shape[2]
    y_span = pencils // x_span
    tall = count * y_span
    tiles = x_span // count
    z_blocks = z_ref.shape[0]
    lag = min(2, tiles)

    barrier = pltpu.get_barrier_semaphore()
    for d in range(1, n_img):
        pl.semaphore_signal(
            barrier, inc=1, device_id={"img": lax.rem(my_img + d, n_img)}, device_id_type=MESH
        )
    for d in range(1, n_ori):
        pl.semaphore_signal(
            barrier, inc=1, device_id={"ori": lax.rem(my_ori + d, n_ori)}, device_id_type=MESH
        )
    pl.semaphore_wait(barrier, n_img + n_ori - 2)

    def rows_of(tile):
        return pl.ds(pl.multiple_of(tile * tall, tall), tall)

    def columns_of(tile):
        return pl.ds(tile * count, count)

    def img_copy(tile, d, slab):
        peer = lax.rem(my_img + d, n_img)
        return pltpu.make_async_remote_copy(
            src_ref=to_img.at[peer, rows_of(tile)],
            dst_ref=from_img.at[slab, rows_of(tile)],
            send_sem=img_send.at[tile, d - 1],
            recv_sem=img_recv.at[tile, d - 1],
            device_id={"img": peer},
            device_id_type=MESH,
        )

    def ori_copy(tile, d, slab):
        peer = lax.rem(my_ori + d, n_ori)
        return pltpu.make_async_remote_copy(
            src_ref=to_ori.at[peer, columns_of(tile)],
            dst_ref=out_ref.at[slab, columns_of(tile)],
            send_sem=ori_send.at[tile, d - 1],
            recv_sem=ori_recv.at[tile, d - 1],
            device_id={"ori": peer},
            device_id_type=MESH,
        )

    def own_copy(tile):
        return pltpu.make_async_copy(
            to_ori.at[my_ori, columns_of(tile)],
            out_ref.at[my_ori, columns_of(tile)],
            own_sem.at[tile],
        )

    def along_z(tile):
        first = (lax.broadcasted_iota(jnp.int32, (tall, depth), 0) + tile * tall) * z_blocks
        result = jnp.zeros((tall, n_img * width), F32)
        for half in range(z_blocks):
            total = jnp.zeros((tall, term_ref.shape[1]), F32)
            for start in range(0, term_ref.shape[0], depth):
                hit = jnp.where(first + half == cell_ref[:, start : start + depth], 1.0, 0.0)
                total += dot(hit.astype(BF16), term_ref[start : start + depth, :])
            total = total.astype(BF16)
            result += dot(total, z_ref[half, 0]) + dot(total, z_ref[half, 1])
        for chunk in range(n_img):
            to_img[chunk, rows_of(tile), :] = result[
                :, chunk * width : (chunk + 1) * width
            ].astype(BF16)
        for d in range(1, n_img):
            img_copy(tile, d, my_img).start()
        from_img[my_img, rows_of(tile), :] = to_img[my_img, rows_of(tile), :]

    def along_y(tile):
        for d in range(1, n_img):
            img_copy(tile, d, lax.rem(my_img - d + n_img, n_img)).wait_recv()
        plain, turned = [], []
        for x in range(count):
            place = pl.ds(pl.multiple_of(tile * tall + x * y_span, y_span), y_span)
            column = jnp.concatenate(
                [from_img[source, place, :] for source in range(n_img)], axis=0
            )
            plain.append(column)
            turned.append(dot(column, turn_ref[...]).astype(BF16))
        plain = jnp.concatenate(plain, axis=1)
        turned = jnp.concatenate(turned, axis=1)
        result = dot(dft_ref[0], plain) + dot(dft_ref[1], plain)
        result += dot(dft_ref[2], turned) + dot(dft_ref[3], turned)
        for x in range(count):
            for target in range(n_ori):
                to_ori[target, tile * count + x] = result[
                    target * y_out : (target + 1) * y_out, x * width : (x + 1) * width
                ].astype(BF16)
        for d in range(1, n_ori):
            ori_copy(tile, d, my_ori).start()
        own_copy(tile).start()

    @pl.loop(0, tiles + lag)
    def _(step):
        @pl.when(step < tiles)
        def _():
            along_z(step)

        @pl.when(step >= lag)
        def _():
            along_y(step - lag)

    @pl.loop(0, tiles)
    def _(tile):
        for d in range(1, n_img):
            img_copy(tile, d, my_img).wait_send()
        for d in range(1, n_ori):
            ori_copy(tile, d, my_ori).wait_send()
            ori_copy(tile, d, lax.rem(my_ori - d + n_ori, n_ori)).wait_recv()
        own_copy(tile).wait()


def x_kernel(dft_ref, in_ref, out_ref, wide, left):
    box, count, width = in_ref.shape
    half = width // 2
    wide[...] = in_ref[...].astype(F32)
    for y in range(count):
        row = wide[:, y, :].T
        left[0, y * width : (y + 1) * width, :] = row.astype(BF16)
        left[1, y * width : (y + 1) * width, :] = jnp.concatenate(
            [-row[half:], row[:half]], axis=0
        ).astype(BF16)
    result = dot(left[0], dft_ref[0]) + dot(left[0], dft_ref[1])
    result += dot(left[1], dft_ref[2]) + dot(left[1], dft_ref[3])
    for y in range(count):
        out_ref[:, y, :] = result[y * width : (y + 1) * width, :]


def whole(shape):
    return pl.BlockSpec(shape, lambda i: (0,) * len(shape))


def combine(pairs):
    peaks, totals = pairs[:, 0], pairs[:, 1]
    peak = jnp.max(peaks, axis=0)
    return peak, jnp.sum(totals * jnp.exp(peaks - peak), axis=0)


def local(
    images, projections, noise_weight, shift_ids, owner_ids, cell_ids, weight_ids, interp_table
):
    n_img, n_ori = lax.axis_size("img"), lax.axis_size("ori")
    devices = n_img * n_ori
    row_count, _, coef_count = images.shape
    shift_count = shift_ids.shape[1]
    orient = projections.shape[0]
    tables, block_len, _ = interp_table.shape
    rows = row_count * shift_count
    blocks = owner_ids.shape[1]
    block_count = orient * blocks
    capacity = max(2, (3 * block_count + devices - 1) // devices)
    slots = devices * capacity

    owners = owner_ids.T.reshape(-1)
    cells = cell_ids.T.reshape(-1)
    group = math.gcd(block_count, 128)
    named = owners[:, None] == jnp.arange(devices, dtype=jnp.int32)[None, :]
    named_b = named.astype(BF16).reshape(-1, group, devices)
    lower = jnp.tril(jnp.ones((group, group), BF16))
    within = jnp.einsum("ij,gjd->gid", lower, named_b, preferred_element_type=F32)
    before = jnp.cumsum(within[:, -1], axis=0) - within[:, -1]
    running = (within + before[:, None, :]).reshape(block_count, devices)
    rank = jnp.sum(jnp.where(named, running, 0.0), axis=1).astype(jnp.int32) - 1
    slot_ids = owners * capacity + rank
    send_cells = (
        jnp.full((slots,), -1, jnp.int32).at[slot_ids].set(cells).reshape(devices, capacity)
    )
    got_cells = lax.all_to_all(
        send_cells, ("img", "ori"), split_axis=0, concat_axis=0, tiled=True
    ).reshape(1, slots)
    ids = jnp.broadcast_to(
        weight_ids.T.astype(BF16)[:, None, :, None], (blocks, 2, orient, block_len)
    )

    chunk = math.gcd(coef_count, 1024)
    steps = coef_count // chunk
    cos_table, sin_table = phase_tables(coef_count)
    depth = cos_table.shape[0]
    pick = (
        shift_ids.T.reshape(-1)[:, None] == jnp.arange(depth, dtype=jnp.int32)[None, :] % 64
    ).astype(BF16)
    image_parts = images.transpose(1, 0, 2)
    proj_parts = projections.transpose(1, 0, 2)
    table_spec = pl.BlockSpec((depth, chunk), lambda i: (0, i))
    image_spec = pl.BlockSpec((2, row_count, chunk), lambda i: (0, 0, i))
    scores, aligned = pl.pallas_call(
        functools.partial(score_kernel, steps),
        grid=(steps,),
        out_shape=(
            jax.ShapeDtypeStruct((rows, orient), F32),
            jax.ShapeDtypeStruct((2, rows, coef_count), BF16),
        ),
        in_specs=[
            whole((rows, depth)),
            table_spec,
            table_spec,
            image_spec,
            pl.BlockSpec((2, orient, chunk), lambda i: (0, 0, i)),
            pl.BlockSpec((1, chunk), lambda i: (0, i)),
        ],
        out_specs=(
            whole((rows, orient)),
            pl.BlockSpec((2, rows, chunk), lambda i: (0, 0, i)),
        ),
        scratch_shapes=[pltpu.VMEM((orient, 128), F32)],
        compiler_params=params(),
        name="scores",
    )(pick, cos_table, sin_table, image_parts, proj_parts, noise_weight.reshape(1, -1))
    scores = scores.reshape(shift_count, row_count, orient)
    local_peak = jnp.max(scores, axis=(0, 2))
    local_total = jnp.sum(jnp.exp(scores - local_peak[None, :, None]), axis=(0, 2))
    peak, total = combine(lax.all_gather(jnp.stack([local_peak, local_total]), "ori"))
    loglik = peak + jnp.log(total)
    prob = (jnp.exp(scores - peak[None, :, None]) / total[None, :, None]).astype(BF16)
    prob = prob.reshape(rows, orient).T

    half_blocks = blocks // 2
    half_chunk = half_blocks * block_len
    half_count = half_blocks * orient
    half_shape = (n_img * half_blocks, 2, orient, block_len)
    group = math.gcd(half_blocks, 4)
    group_shape = (group, 2, orient, block_len)
    flat_table = interp_table.reshape(tables * block_len, block_len)
    halves = []
    for half in range(2):
        partial_sums = pl.pallas_call(
            slice_kernel,
            grid=(n_img,),
            out_shape=jax.ShapeDtypeStruct(half_shape, BF16),
            in_specs=[
                pl.BlockSpec((2, rows, half_chunk), lambda i, half=half: (0, 0, 2 * i + half)),
                whole((orient, rows)),
            ],
            out_specs=pl.BlockSpec((half_blocks, 2, orient, block_len), lambda i: (i, 0, 0, 0)),
            compiler_params=params(),
            cost_estimate=cost(2 * orient * rows * coef_count, 2 * rows * coef_count),
            name="slices",
        )(aligned, prob)
        halves.append(lax.psum_scatter(partial_sums, "img", scatter_dimension=0, tiled=True))
    terms = []
    for half in range(2):
        offset = half * (half_blocks // group)
        terms.append(
            pl.pallas_call(
                functools.partial(interp_kernel, tables),
                grid=(half_blocks // group,),
                out_shape=jax.ShapeDtypeStruct((half_count, 2 * block_len), BF16),
                in_specs=[
                    pl.BlockSpec(group_shape, lambda i: (i, 0, 0, 0)),
                    pl.BlockSpec(group_shape, lambda i, offset=offset: (i + offset, 0, 0, 0)),
                    whole(flat_table.shape),
                ],
                out_specs=pl.BlockSpec((group * orient, 2 * block_len), lambda i: (i, 0)),
                compiler_params=params(),
                cost_estimate=cost(
                    8 * half_count * tables * block_len * block_len, 4 * half_count * block_len
                ),
                name="interpolate",
            )(halves[half], ids, flat_table)
        )

    tile = math.gcd(slots, 512)
    send_terms = pl.pallas_call(
        place_kernel,
        grid=(slots // tile,),
        out_shape=jax.ShapeDtypeStruct((slots, 2 * block_len), BF16),
        in_specs=[whole((1, block_count))] + [whole((half_count, 2 * block_len))] * 2,
        out_specs=pl.BlockSpec((tile, 2 * block_len), lambda i: (i, 0)),
        compiler_params=params(),
        name="place",
    )(slot_ids.reshape(1, block_count), *terms)
    got_terms = lax.all_to_all(
        send_terms.reshape(devices, capacity, 2 * block_len),
        ("img", "ori"),
        split_axis=0,
        concat_axis=0,
        tiled=True,
    ).reshape(slots, 2 * block_len)

    x_span, y_span, y_out = BOX // n_ori, BOX // n_img, BOX // n_ori
    pencils = x_span * y_span
    width = 2 * (BOX // n_img)
    z_table = z_tables(block_len, n_img)
    dft = cos_sin_split()
    count = math.gcd(x_span, 4)
    tiles = x_span // count
    vmem = pl.BlockSpec(memory_space=pltpu.VMEM)
    pencil_parts = pl.pallas_call(
        functools.partial(transform_kernel, n_img, n_ori, count, math.gcd(slots, 2048)),
        out_shape=jax.ShapeDtypeStruct((n_ori, x_span, y_out, width), BF16),
        in_specs=[vmem] * 5,
        out_specs=pl.BlockSpec(memory_space=pl.ANY),
        scratch_shapes=[
            pltpu.VMEM((n_img, pencils, width), BF16),
            pltpu.VMEM((n_img, pencils, width), BF16),
            pltpu.VMEM((n_ori, x_span, y_out, width), BF16),
            pltpu.SemaphoreType.DMA((tiles, n_img - 1)),
            pltpu.SemaphoreType.DMA((tiles, n_img - 1)),
            pltpu.SemaphoreType.DMA((tiles, n_ori - 1)),
            pltpu.SemaphoreType.DMA((tiles, n_ori - 1)),
            pltpu.SemaphoreType.DMA((tiles,)),
        ],
        compiler_params=params(collective_id=0, has_side_effects=True),
        name="transform",
    )(got_cells, got_terms, z_table, dft, turn_table(width))

    count = math.gcd(y_out, 16)
    realspace = pl.pallas_call(
        x_kernel,
        grid=(y_out // count,),
        out_shape=jax.ShapeDtypeStruct((width, y_out, BOX), F32),
        in_specs=[
            whole(dft.shape),
            pl.BlockSpec((BOX, count, width), lambda i: (0, i, 0)),
        ],
        out_specs=pl.BlockSpec((width, count, BOX), lambda i: (0, i, 0)),
        scratch_shapes=[
            pltpu.VMEM((BOX, count, width), F32),
            pltpu.VMEM((2, count * width, BOX), BF16),
        ],
        compiler_params=params(),
        name="along_x",
    )(dft, pencil_parts.reshape(BOX, y_out, width))
    return realspace.reshape(2, width // 2, y_out, BOX), loglik


def solution(mesh):
    placed = (
        P("img", None, None),
        P("ori", None, None),
        P(),
        P("img", None),
        P("ori", "img"),
        P("ori", "img"),
        P("ori", "img"),
        P(),
    )
    return jax.shard_map(
        local,
        mesh=mesh,
        in_specs=placed,
        out_specs=(P(None, "img", "ori", None), P("img")),
        check_vma=False,
    )
```

```python
import functools
import math

import jax
import jax.numpy as jnp
import ml_dtypes
import numpy as np
from jax import lax
from jax.experimental import pallas as pl
from jax.experimental.pallas import tpu as pltpu
from jax.sharding import PartitionSpec as P

IMGBOX = 128
BOX = 256
GRID = 7
VMEM_BYTES = 56 * 1024 * 1024
F32 = jnp.float32
BF16 = jnp.bfloat16
MESH = pl.DeviceIdType.MESH


def split_table(table, terms):
    rest = table.astype(np.float32)
    pieces = []
    for _ in range(terms):
        piece = rest.astype(ml_dtypes.bfloat16)
        pieces.append(piece)
        rest = rest - piece.astype(np.float32)
    return pieces


def phase_tables(coef_count):
    coef = np.arange(coef_count)
    kx, ky = coef % IMGBOX - IMGBOX // 2, coef // IMGBOX
    shift = np.arange(64)
    dx, dy = shift % GRID - GRID // 2, shift // GRID - GRID // 2
    turns = (kx[None, :] * dx[:, None] + ky[None, :] * dy[:, None]) % IMGBOX
    angles = turns * (-2.0 * math.pi / IMGBOX)
    return (
        np.concatenate(split_table(np.cos(angles), 3)),
        np.concatenate(split_table(np.sin(angles), 3)),
    )


def dft_tables():
    index = np.arange(BOX)
    angles = (index[:, None] * index[None, :] % BOX) * (2.0 * math.pi / BOX)
    factor = 1.0 / math.sqrt(BOX)
    return np.cos(angles) * factor, np.sin(angles) * factor


def z_tables(block_len, chunks):
    cosine, sine = dft_tables()
    span = BOX // chunks
    full = np.zeros((2, BOX, chunks, 2, span))
    cos_c, sin_c = cosine.reshape(BOX, chunks, span), sine.reshape(BOX, chunks, span)
    full[0, :, :, 0], full[0, :, :, 1] = cos_c, sin_c
    full[1, :, :, 0], full[1, :, :, 1] = -sin_c, cos_c
    full = full.reshape(2, BOX // block_len, block_len, 2 * BOX).transpose(1, 0, 2, 3)
    full = full.reshape(BOX // block_len, 2 * block_len, 2 * BOX)
    return np.stack(split_table(full, 2), axis=1)


def cos_sin_split():
    cosine, sine = dft_tables()
    return np.stack(split_table(cosine, 2) + split_table(sine, 2))


def turn_table(width):
    half = width // 2
    table = np.zeros((width, width), np.float32)
    for j in range(half):
        table[j, half + j] = 1.0
        table[half + j, j] = -1.0
    return table.astype(ml_dtypes.bfloat16)


def dot(left, right):
    return jnp.dot(left, right, preferred_element_type=F32)


def params(**more):
    return pltpu.CompilerParams(vmem_limit_bytes=VMEM_BYTES, **more)


def aligned_chunk(pick, cos_ref, sin_ref, img_ref):
    cosine = dot(pick, cos_ref[...])
    sine = dot(pick, sin_ref[...])
    real = img_ref[0].astype(F32)
    imag = img_ref[1].astype(F32)
    new_real = (real * cosine - imag * sine).astype(BF16)
    new_imag = (real * sine + imag * cosine).astype(BF16)
    return new_real, new_imag


def score_kernel(
    steps, pick_ref, cos_ref, sin_ref, img_ref, proj_ref, noise_ref, out_ref, aligned_ref, norm
):
    step = pl.program_id(0)
    rows = img_ref.shape[1]
    chunk = img_ref.shape[2]

    @pl.when(step == 0)
    def _():
        out_ref[...] = jnp.zeros_like(out_ref)
        norm[...] = jnp.zeros_like(norm)

    noise = noise_ref[...]
    weighted = []
    for part in range(2):
        proj = proj_ref[part].astype(F32)
        scaled = proj * noise
        weighted.append(scaled.astype(BF16))
        power = scaled * proj
        for lane in range(0, chunk, 128):
            norm[...] += power[:, lane : lane + 128]
    dims = (((1,), (1,)), ((), ()))
    for group in range(pick_ref.shape[0] // rows):
        span = pl.ds(group * rows, rows)
        real, imag = aligned_chunk(pick_ref[span, :], cos_ref, sin_ref, img_ref)
        aligned_ref[0, span, :] = real
        aligned_ref[1, span, :] = imag
        out_ref[span, :] += lax.dot_general(
            real, weighted[0], dims, preferred_element_type=F32
        ) + lax.dot_general(imag, weighted[1], dims, preferred_element_type=F32)

    @pl.when(step == steps - 1)
    def _():
        out_ref[...] -= 0.5 * jnp.sum(norm[...].T, axis=0, keepdims=True)


def slice_kernel(
    n_img,
    subs,
    tables,
    aligned_ref,
    prob_ref,
    id_ref,
    table_ref,
    out_ref,
    to_peer,
    from_peer,
    send_sem,
    recv_sem,
):
    step = pl.program_id(0)
    sub, target = step // n_img, step % n_img
    me = lax.axis_index("img")
    _, _, group, _, orient, block_len = to_peer.shape

    @pl.when(step == 0)
    def _():
        barrier = pltpu.get_barrier_semaphore()
        for d in range(1, n_img):
            pl.semaphore_signal(
                barrier, inc=1, device_id={"img": lax.rem(me + d, n_img)}, device_id_type=MESH
            )
        pl.semaphore_wait(barrier, n_img - 1)

    def peer_copy(part_index, peer, slab):
        return pltpu.make_async_remote_copy(
            src_ref=to_peer.at[part_index, peer],
            dst_ref=from_peer.at[part_index, slab],
            send_sem=send_sem.at[part_index, peer],
            recv_sem=recv_sem.at[part_index, slab],
            device_id={"img": peer},
            device_id_type=MESH,
        )

    for part in range(2):
        total = dot(prob_ref[...], aligned_ref[part])
        for block in range(group):
            piece = total[:, block * block_len : (block + 1) * block_len]
            to_peer[sub, target, block, part] = piece.astype(BF16)

    @pl.when(target != me)
    def _():
        peer_copy(sub, target, me).start()

    @pl.when(step == subs * n_img - 1)
    def _():
        @pl.loop(0, subs)
        def _(index):
            from_peer[index, me] = to_peer[index, me]
            for d in range(1, n_img):
                source = lax.rem(me + d, n_img)
                peer_copy(index, source, source).wait_recv()
            summed = from_peer[index, 0].astype(F32)
            for source in range(1, n_img):
                summed += from_peer[index, source].astype(F32)
            values = summed.astype(BF16).reshape(group * 2 * orient, block_len)
            ids = id_ref[pl.ds(index * group, group)].reshape(group * 2 * orient, block_len)
            batch = math.gcd(tables, 8)
            total = jnp.zeros(values.shape, F32)
            for first in range(0, tables, batch):
                picked = [
                    jnp.where(ids == jnp.asarray(w, BF16), values, jnp.zeros_like(values))
                    for w in range(first, first + batch)
                ]
                total += dot(
                    jnp.concatenate(picked, axis=1),
                    table_ref[first * block_len : (first + batch) * block_len, :],
                )
            total = total.astype(BF16).reshape(group, 2, orient, block_len)
            for block in range(group):
                place = pl.multiple_of((index * group + block) * orient, orient)
                for part in range(2):
                    lanes = slice(part * block_len, (part + 1) * block_len)
                    out_ref[pl.ds(place, orient), lanes] = total[block, part]

        @pl.loop(0, subs)
        def _(index):
            for d in range(1, n_img):
                peer_copy(index, lax.rem(me + d, n_img), me).wait_send()


def place_kernel(slot_ref, term_ref, out_ref):
    step = pl.program_id(0)
    rows = out_ref.shape[0]
    wanted = lax.broadcasted_iota(jnp.int32, (rows, term_ref.shape[0]), 0) + step * rows
    hit = jnp.where(wanted == slot_ref[...], 1.0, 0.0).astype(BF16)
    out_ref[...] = dot(hit, term_ref[...]).astype(BF16)


def transform_kernel(
    n_img,
    n_ori,
    count,
    depth,
    cell_ref,
    term_ref,
    z_ref,
    dft_ref,
    turn_ref,
    out_ref,
    to_img,
    from_img,
    to_ori,
    img_send,
    img_recv,
    ori_send,
    ori_recv,
    own_sem,
):
    my_img, my_ori = lax.axis_index("img"), lax.axis_index("ori")
    _, pencils, width = to_img.shape
    x_span, y_out = to_ori.shape[1], to_ori.shape[2]
    y_span = pencils // x_span
    tall = count * y_span
    tiles = x_span // count
    z_blocks = z_ref.shape[0]
    lag = min(2, tiles)

    barrier = pltpu.get_barrier_semaphore()
    for d in range(1, n_img):
        pl.semaphore_signal(
            barrier, inc=1, device_id={"img": lax.rem(my_img + d, n_img)}, device_id_type=MESH
        )
    for d in range(1, n_ori):
        pl.semaphore_signal(
            barrier, inc=1, device_id={"ori": lax.rem(my_ori + d, n_ori)}, device_id_type=MESH
        )
    pl.semaphore_wait(barrier, n_img + n_ori - 2)

    def rows_of(tile):
        return pl.ds(pl.multiple_of(tile * tall, tall), tall)

    def columns_of(tile):
        return pl.ds(tile * count, count)

    def img_copy(tile, d, slab):
        peer = lax.rem(my_img + d, n_img)
        return pltpu.make_async_remote_copy(
            src_ref=to_img.at[peer, rows_of(tile)],
            dst_ref=from_img.at[slab, rows_of(tile)],
            send_sem=img_send.at[tile, d - 1],
            recv_sem=img_recv.at[tile, d - 1],
            device_id={"img": peer},
            device_id_type=MESH,
        )

    def ori_copy(tile, d, slab):
        peer = lax.rem(my_ori + d, n_ori)
        return pltpu.make_async_remote_copy(
            src_ref=to_ori.at[peer, columns_of(tile)],
            dst_ref=out_ref.at[slab, columns_of(tile)],
            send_sem=ori_send.at[tile, d - 1],
            recv_sem=ori_recv.at[tile, d - 1],
            device_id={"ori": peer},
            device_id_type=MESH,
        )

    def own_copy(tile):
        return pltpu.make_async_copy(
            to_ori.at[my_ori, columns_of(tile)],
            out_ref.at[my_ori, columns_of(tile)],
            own_sem.at[tile],
        )

    def along_z(tile):
        first = (lax.broadcasted_iota(jnp.int32, (tall, depth), 0) + tile * tall) * z_blocks
        result = jnp.zeros((tall, n_img * width), F32)
        for half in range(z_blocks):
            total = jnp.zeros((tall, term_ref.shape[1]), F32)
            for start in range(0, term_ref.shape[0], depth):
                hit = jnp.where(first + half == cell_ref[:, start : start + depth], 1.0, 0.0)
                total += dot(hit.astype(BF16), term_ref[start : start + depth, :])
            total = total.astype(BF16)
            result += dot(total, z_ref[half, 0]) + dot(total, z_ref[half, 1])
        for chunk in range(n_img):
            to_img[chunk, rows_of(tile), :] = result[
                :, chunk * width : (chunk + 1) * width
            ].astype(BF16)
        for d in range(1, n_img):
            img_copy(tile, d, my_img).start()
        from_img[my_img, rows_of(tile), :] = to_img[my_img, rows_of(tile), :]

    def along_y(tile):
        for d in range(1, n_img):
            img_copy(tile, d, lax.rem(my_img - d + n_img, n_img)).wait_recv()
        plain, turned = [], []
        for x in range(count):
            place = pl.ds(pl.multiple_of(tile * tall + x * y_span, y_span), y_span)
            column = jnp.concatenate(
                [from_img[source, place, :] for source in range(n_img)], axis=0
            )
            plain.append(column)
            turned.append(dot(column, turn_ref[...]).astype(BF16))
        plain = jnp.concatenate(plain, axis=1)
        turned = jnp.concatenate(turned, axis=1)
        result = dot(dft_ref[0], plain) + dot(dft_ref[1], plain)
        result += dot(dft_ref[2], turned) + dot(dft_ref[3], turned)
        for x in range(count):
            for target in range(n_ori):
                to_ori[target, tile * count + x] = result[
                    target * y_out : (target + 1) * y_out, x * width : (x + 1) * width
                ].astype(BF16)
        for d in range(1, n_ori):
            ori_copy(tile, d, my_ori).start()
        own_copy(tile).start()

    @pl.loop(0, tiles + lag)
    def _(step):
        @pl.when(step < tiles)
        def _():
            along_z(step)

        @pl.when(step >= lag)
        def _():
            along_y(step - lag)

    @pl.loop(0, tiles)
    def _(tile):
        for d in range(1, n_img):
            img_copy(tile, d, my_img).wait_send()
        for d in range(1, n_ori):
            ori_copy(tile, d, my_ori).wait_send()
            ori_copy(tile, d, lax.rem(my_ori - d + n_ori, n_ori)).wait_recv()
        own_copy(tile).wait()


def x_kernel(dft_ref, in_ref, out_ref, wide, left):
    box, count, width = in_ref.shape
    half = width // 2
    wide[...] = in_ref[...].astype(F32)
    for y in range(count):
        row = wide[:, y, :].T
        left[0, y * width : (y + 1) * width, :] = row.astype(BF16)
        left[1, y * width : (y + 1) * width, :] = jnp.concatenate(
            [-row[half:], row[:half]], axis=0
        ).astype(BF16)
    result = dot(left[0], dft_ref[0]) + dot(left[0], dft_ref[1])
    result += dot(left[1], dft_ref[2]) + dot(left[1], dft_ref[3])
    for y in range(count):
        out_ref[:, y, :] = result[y * width : (y + 1) * width, :]


def whole(shape):
    return pl.BlockSpec(shape, lambda i: (0,) * len(shape))


def combine(pairs):
    peaks, totals = pairs[:, 0], pairs[:, 1]
    peak = jnp.max(peaks, axis=0)
    return peak, jnp.sum(totals * jnp.exp(peaks - peak), axis=0)


def local(
    images, projections, noise_weight, shift_ids, owner_ids, cell_ids, weight_ids, interp_table
):
    n_img, n_ori = lax.axis_size("img"), lax.axis_size("ori")
    devices = n_img * n_ori
    row_count, _, coef_count = images.shape
    shift_count = shift_ids.shape[1]
    orient = projections.shape[0]
    tables, block_len, _ = interp_table.shape
    rows = row_count * shift_count
    blocks = owner_ids.shape[1]
    block_count = orient * blocks
    capacity = max(2, (3 * block_count + devices - 1) // devices)
    slots = devices * capacity

    owners = owner_ids.T.reshape(-1)
    cells = cell_ids.T.reshape(-1)
    group = math.gcd(block_count, 128)
    named = owners[:, None] == jnp.arange(devices, dtype=jnp.int32)[None, :]
    named_b = named.astype(BF16).reshape(-1, group, devices)
    lower = jnp.tril(jnp.ones((group, group), BF16))
    within = jnp.einsum("ij,gjd->gid", lower, named_b, preferred_element_type=F32)
    before = jnp.cumsum(within[:, -1], axis=0) - within[:, -1]
    running = (within + before[:, None, :]).reshape(block_count, devices)
    rank = jnp.sum(jnp.where(named, running, 0.0), axis=1).astype(jnp.int32) - 1
    slot_ids = owners * capacity + rank
    send_cells = (
        jnp.full((slots,), -1, jnp.int32).at[slot_ids].set(cells).reshape(devices, capacity)
    )
    ids = jnp.broadcast_to(
        weight_ids.T.astype(BF16)[:, None, :, None], (blocks, 2, orient, block_len)
    )

    chunk = math.gcd(coef_count, 1024)
    steps = coef_count // chunk
    cos_table, sin_table = phase_tables(coef_count)
    depth = cos_table.shape[0]
    pick = (
        shift_ids.T.reshape(-1)[:, None] == jnp.arange(depth, dtype=jnp.int32)[None, :] % 64
    ).astype(BF16)
    image_parts = images.transpose(1, 0, 2)
    proj_parts = projections.transpose(1, 0, 2)
    table_spec = pl.BlockSpec((depth, chunk), lambda i: (0, i))
    image_spec = pl.BlockSpec((2, row_count, chunk), lambda i: (0, 0, i))
    scores, aligned = pl.pallas_call(
        functools.partial(score_kernel, steps),
        grid=(steps,),
        out_shape=(
            jax.ShapeDtypeStruct((rows, orient), F32),
            jax.ShapeDtypeStruct((2, rows, coef_count), BF16),
        ),
        in_specs=[
            whole((rows, depth)),
            table_spec,
            table_spec,
            image_spec,
            pl.BlockSpec((2, orient, chunk), lambda i: (0, 0, i)),
            pl.BlockSpec((1, chunk), lambda i: (0, i)),
        ],
        out_specs=(
            whole((rows, orient)),
            pl.BlockSpec((2, rows, chunk), lambda i: (0, 0, i)),
        ),
        scratch_shapes=[pltpu.VMEM((orient, 128), F32)],
        compiler_params=params(),
        name="scores",
    )(pick, cos_table, sin_table, image_parts, proj_parts, noise_weight.reshape(1, -1))
    scores = scores.reshape(shift_count, row_count, orient)
    local_peak = jnp.max(scores, axis=(0, 2))
    local_total = jnp.sum(jnp.exp(scores - local_peak[None, :, None]), axis=(0, 2))
    pairs = lax.all_gather(jnp.stack([local_peak, local_total]), "ori")
    pairs, send_cells, slot_ids, ids = lax.optimization_barrier(
        (pairs, send_cells, slot_ids, ids)
    )
    got_cells = lax.all_to_all(
        send_cells, ("img", "ori"), split_axis=0, concat_axis=0, tiled=True
    ).reshape(1, slots)
    peak, total = combine(pairs)
    loglik = peak + jnp.log(total)
    prob = (jnp.exp(scores - peak[None, :, None]) / total[None, :, None]).astype(BF16)
    prob = prob.reshape(rows, orient).T

    group = math.gcd(blocks, 4)
    subs = blocks // group
    flat_table = interp_table.reshape(tables * block_len, block_len)
    exchange = (subs, n_img, group, 2, orient, block_len)
    terms = pl.pallas_call(
        functools.partial(slice_kernel, n_img, subs, tables),
        grid=(subs * n_img,),
        out_shape=jax.ShapeDtypeStruct((block_count, 2 * block_len), BF16),
        in_specs=[
            pl.BlockSpec(
                (2, rows, group * block_len), lambda i: (0, 0, i % n_img * subs + i // n_img)
            ),
            whole((orient, rows)),
            whole(ids.shape),
            whole(flat_table.shape),
        ],
        out_specs=whole((block_count, 2 * block_len)),
        scratch_shapes=[
            pltpu.VMEM(exchange, BF16),
            pltpu.VMEM(exchange, BF16),
            pltpu.SemaphoreType.DMA((subs, n_img)),
            pltpu.SemaphoreType.DMA((subs, n_img)),
        ],
        compiler_params=params(collective_id=1, has_side_effects=True),
        name="slices",
    )(aligned, prob, ids, flat_table)

    tile = math.gcd(slots, 512)
    send_terms = pl.pallas_call(
        place_kernel,
        grid=(slots // tile,),
        out_shape=jax.ShapeDtypeStruct((slots, 2 * block_len), BF16),
        in_specs=[whole((1, block_count)), whole((block_count, 2 * block_len))],
        out_specs=pl.BlockSpec((tile, 2 * block_len), lambda i: (i, 0)),
        compiler_params=params(),
        name="place",
    )(slot_ids.reshape(1, block_count), terms)
    got_terms = lax.all_to_all(
        send_terms.reshape(devices, capacity, 2 * block_len),
        ("img", "ori"),
        split_axis=0,
        concat_axis=0,
        tiled=True,
    ).reshape(slots, 2 * block_len)

    x_span, y_span, y_out = BOX // n_ori, BOX // n_img, BOX // n_ori
    pencils = x_span * y_span
    width = 2 * (BOX // n_img)
    z_table = z_tables(block_len, n_img)
    dft = cos_sin_split()
    count = math.gcd(x_span, 4)
    tiles = x_span // count
    vmem = pl.BlockSpec(memory_space=pltpu.VMEM)
    pencil_parts = pl.pallas_call(
        functools.partial(transform_kernel, n_img, n_ori, count, math.gcd(slots, 2048)),
        out_shape=jax.ShapeDtypeStruct((n_ori, x_span, y_out, width), BF16),
        in_specs=[vmem] * 5,
        out_specs=pl.BlockSpec(memory_space=pl.ANY),
        scratch_shapes=[
            pltpu.VMEM((n_img, pencils, width), BF16),
            pltpu.VMEM((n_img, pencils, width), BF16),
            pltpu.VMEM((n_ori, x_span, y_out, width), BF16),
            pltpu.SemaphoreType.DMA((tiles, n_img - 1)),
            pltpu.SemaphoreType.DMA((tiles, n_img - 1)),
            pltpu.SemaphoreType.DMA((tiles, n_ori - 1)),
            pltpu.SemaphoreType.DMA((tiles, n_ori - 1)),
            pltpu.SemaphoreType.DMA((tiles,)),
        ],
        compiler_params=params(collective_id=0, has_side_effects=True),
        name="transform",
    )(got_cells, got_terms, z_table, dft, turn_table(width))

    count = math.gcd(y_out, 16)
    realspace = pl.pallas_call(
        x_kernel,
        grid=(y_out // count,),
        out_shape=jax.ShapeDtypeStruct((width, y_out, BOX), F32),
        in_specs=[
            whole(dft.shape),
            pl.BlockSpec((BOX, count, width), lambda i: (0, i, 0)),
        ],
        out_specs=pl.BlockSpec((width, count, BOX), lambda i: (0, i, 0)),
        scratch_shapes=[
            pltpu.VMEM((BOX, count, width), F32),
            pltpu.VMEM((2, count * width, BOX), BF16),
        ],
        compiler_params=params(),
        name="along_x",
    )(dft, pencil_parts.reshape(BOX, y_out, width))
    return realspace.reshape(2, width // 2, y_out, BOX), loglik


def solution(mesh):
    placed = (
        P("img", None, None),
        P("ori", None, None),
        P(),
        P("img", None),
        P("ori", "img"),
        P("ori", "img"),
        P("ori", "img"),
        P(),
    )
    return jax.shard_map(
        local,
        mesh=mesh,
        in_specs=placed,
        out_specs=(P(None, "img", "ori", None), P("img")),
        check_vma=False,
    )
```
